32 devices in a mesh: lon: 16 (over z, x, core), lat: 2 (over y).
Axes of the slice: x: 2, y: 2, z: 4, core: 2. Of those that a mesh axis runs over, the one named last changes fastest.
Arguments:
- tracer: float32 [8, 256, 4096], P(None, 'lat', 'lon'), may hold values from -6 to 6
- u_vel: float32 [8, 256, 4096], P(None, 'lat', 'lon'), may hold values from -6 to 6
- v_vel: float32 [8, 256, 4096], P(None, 'lat', 'lon'), may hold values from -6 to 6
- surface: float32 [256, 4096], P('lat', 'lon'), may hold values from -6 to 6
- land_mask: int32 [8, 256, 4096], P(None, 'lat', 'lon'), may hold values 0 or 1
- bottom: int32 [256, 4096], P('lat', 'lon'), may hold values from 1 to 8
- w_in: bfloat16 [24, 128], replicated, may hold values from -1.25 to 1.25
- b_in: float32 [128], replicated, may hold values from -4 to 4
- w_mid: bfloat16 [128, 128], replicated, may hold values from -0.5 to 0.5
- b_mid: float32 [128], replicated, may hold values from -4 to 4
- w_out: bfloat16 [128, 8], replicated, may hold values from -0.5 to 0.5
Outputs:
- tracer_new: float32 [8, 256, 4096], P(None, 'lat', 'lon')
- u_new: float32 [8, 256, 4096], P(None, 'lat', 'lon')
- v_new: float32 [8, 256, 4096], P(None, 'lat', 'lon')
- surface_new: float32 [256, 4096], P('lat', 'lon')
The draws below stay inside these ranges and needn't reach their ends.
All inputs are finite; a program needn't handle non-finite values. No bound on the sum of `land_mask` on one device may be relied on, other than what follows from the above.
Results may differ from the reference program's by a relative error of at most 0.00034.
Values sent between devices are 32-bit elements; how exact they have to be, the bound alone decides.
A program may use at most 128 MiB of HBM per device.

```python
import jax
import jax.numpy as jnp
from jax import lax

LEV = 8
HID = 128
ITERS = 3
NX = 4096
NY = 256


def set_ends(values, key, low, high):
    longest = values.shape.index(max(values.shape))
    spots = []
    for shift in (0, 1):
        where = [jax.random.randint(jax.random.fold_in(key, axis), (), 0, length) for axis, length in enumerate(values.shape)]
        where[longest] = (where[longest] + shift) % values.shape[longest]
        spots.append(tuple(where))
    return values.at[spots[0]].set(low).at[spots[1]].set(high)


def shard_levels(key, shape, shards, low, top_value):
    def one(axis_at, blocks):
        steps = jax.random.uniform(jax.random.fold_in(jax.random.fold_in(key, 6), axis_at), (blocks,), jnp.float32, low / len(shards), top_value / len(shards))
        return jnp.repeat(jnp.exp(steps), shape[axis_at] // blocks).reshape((-1,) + (1,) * (len(shape) - axis_at - 1))

    loudness = one(*shards[0])
    for cut in shards[1:]:
        loudness = loudness * one(*cut)
    return loudness


def normal_values(own_key, extent, spread, most, split=(), kind=jnp.bfloat16):
    level = shard_levels(own_key, extent, split, -0.22, 0.18) if split else 1.0
    drawn = jax.random.normal(own_key, extent, jnp.float32) * spread * level
    return jnp.minimum(jnp.maximum(drawn, -most), most).astype(kind)


def setup_inputs(seed: int = 0) -> dict:
    keys = jax.random.split(jax.random.key(seed), 12)
    tracer = normal_values(keys[0], (LEV, NY, NX), 1.0, 6.0, ((1, 2), (2, 16)), jnp.float32)
    u_vel = normal_values(keys[1], (LEV, NY, NX), 1.0, 6.0, ((1, 2), (2, 16)), jnp.float32)
    v_vel = normal_values(keys[2], (LEV, NY, NX), 1.0, 6.0, ((1, 2), (2, 16)), jnp.float32)
    surface = normal_values(keys[3], (NY, NX), 1.0, 6.0, ((0, 2), (1, 16)), jnp.float32)
    land_mask = set_ends((jax.random.randint(keys[4], (LEV, NY, NX), 0, 4) < 3).astype(jnp.int32), jax.random.fold_in(keys[4], 1), 0, 1)
    bottom = set_ends(jax.random.randint(keys[5], (NY, NX), 1, LEV + 1), jax.random.fold_in(keys[5], 1), 1, LEV).astype(jnp.int32)
    w_in = normal_values(keys[6], (3 * LEV, HID), (3 * LEV) ** -0.5, 1.25)
    b_in = normal_values(keys[7], (HID,), 0.8, 4.0, (), jnp.float32)
    w_mid = normal_values(keys[8], (HID, HID), HID ** -0.5, 0.5)
    b_mid = normal_values(keys[9], (HID,), 0.8, 4.0, (), jnp.float32)
    w_out = normal_values(keys[10], (HID, LEV), HID ** -0.5, 0.5)
    return {"tracer": tracer, "u_vel": u_vel, "v_vel": v_vel, "surface": surface, "land_mask": land_mask, "bottom": bottom, "w_in": w_in, "b_in": b_in, "w_mid": w_mid, "b_mid": b_mid, "w_out": w_out}


def east(a):
    return jnp.roll(a, -1, axis=-1)


def west(a):
    return jnp.roll(a, 1, axis=-1)


def north(a):
    return jnp.concatenate([a[..., 1:, :], jnp.zeros_like(a[..., :1, :])], axis=-2)


def south(a):
    return jnp.concatenate([jnp.zeros_like(a[..., :1, :]), a[..., :-1, :]], axis=-2)


def reference(tracer, u_vel, v_vel, surface, land_mask, bottom, w_in, b_in, w_mid, b_mid, w_out):
    level_ids = jnp.arange(LEV, dtype=jnp.int32)[:, None, None]
    wet = (land_mask * (level_ids < bottom[None]).astype(jnp.int32)).astype(jnp.float32)
    depth = jnp.sum(wet, axis=0)
    lap = east(wet) * (east(tracer) - tracer) + west(wet) * (west(tracer) - tracer)
    lap = lap + north(wet) * (north(tracer) - tracer) + south(wet) * (south(tracer) - tracer)
    masked = wet * tracer
    adv = -0.5 * (u_vel * (east(masked) - west(masked)) + v_vel * (north(masked) - south(masked)))
    features = jnp.concatenate([tracer, u_vel, v_vel], axis=0).astype(jnp.bfloat16)
    by_rows = jnp.transpose(features, (1, 0, 2))

    def network(row_feats):
        first = jnp.dot(w_in.T, row_feats, preferred_element_type=jnp.float32)
        hidden_one = jnp.tanh(first + b_in[:, None]).astype(jnp.bfloat16)
        second = jnp.dot(w_mid.T, hidden_one, preferred_element_type=jnp.float32)
        hidden_two = jnp.tanh(second + b_mid[:, None]).astype(jnp.bfloat16)
        return jnp.dot(w_out.T, hidden_two, preferred_element_type=jnp.float32)

    closure = jnp.transpose(lax.map(network, by_rows), (1, 0, 2))
    tracer_new = tracer + 0.2 * wet * (lap + adv + closure)
    rows = jnp.arange(NY, dtype=jnp.int32).astype(jnp.float32)
    coriolis = (2.0 * (rows + 0.5) / NY - 1.0)[:, None]
    floor = (level_ids == (bottom[None] - 1)).astype(jnp.float32)
    u_star = u_vel + 0.2 * wet * (coriolis * v_vel - 0.5 * floor * u_vel)
    v_star = v_vel + 0.2 * wet * (-coriolis * u_vel - 0.5 * floor * v_vel)
    trans_u = jnp.sum(wet * u_star, axis=0)
    trans_v = jnp.sum(wet * v_star, axis=0)
    div = 0.5 * (east(trans_u) - west(trans_u) + north(trans_v) - south(trans_v))
    face_e = jnp.minimum(depth, east(depth))
    face_w = jnp.minimum(depth, west(depth))
    face_n = jnp.minimum(depth, north(depth))
    face_s = jnp.minimum(depth, south(depth))

    def operate(x):
        out = x + face_e * (x - east(x)) + face_w * (x - west(x))
        return out + face_n * (x - north(x)) + face_s * (x - south(x))

    precond = 1.0 + face_e + face_w + face_n + face_s
    rhs = surface - div
    x = surface
    resid = rhs - operate(x)
    z = resid / precond
    p = z
    rz = jnp.sum(resid * z)
    for step in range(ITERS):
        q = operate(p)
        alpha = rz / jnp.sum(p * q)
        x = x + alpha * p
        resid = resid - alpha * q
        z = resid / precond
        rz_new = jnp.sum(resid * z)
        p = z + (rz_new / rz) * p
        rz = rz_new
    u_new = wet * (u_star - 0.5 * (east(x) - west(x)))
    v_new = wet * (v_star - 0.5 * (north(x) - south(x)))
    return tracer_new, u_new, v_new, x
```

```python
import functools

import jax
import jax.numpy as jnp
from jax import lax
from jax.experimental import pallas as pl
from jax.experimental.pallas import tpu as pltpu
from jax.sharding import PartitionSpec as P

MESH = pl.DeviceIdType.MESH
HALO = 4
F32 = jnp.float32
BF16 = jnp.bfloat16
NT = (((1,), (1,)), ((), ()))
TN = (((0,), (0,)), ((), ()))


def shift_to(x, offset, axis):
    return pltpu.roll(x, (-offset) % x.shape[axis], axis)


def inner(a, b, moments):
    out = None
    for i, ai in enumerate(a):
        for j, bj in enumerate(b):
            term = ai * bj * moments[i + j]
            out = term if out is None else out + term
    return out


def scaled_minus_shift(p):
    out = [p[0]]
    for lower, upper in zip(p[:-1], p[1:]):
        out.append(upper - lower)
    out.append(-p[-1])
    return out


def add_poly(a, scale, b):
    out = []
    for i in range(max(len(a), len(b))):
        if i >= len(a):
            out.append(scale * b[i])
        elif i >= len(b):
            out.append(a[i])
        else:
            out.append(a[i] + scale * b[i])
    return out


def cg_coefficients(moments, iters, top):
    one = jnp.ones_like(moments[0])
    z, p, x = [one], [one], [jnp.zeros_like(one)]
    rz = moments[0]
    for step in range(iters):
        q = scaled_minus_shift(p)
        pq = jnp.maximum(inner(p, q, moments), rz * (1.0 / top))
        alpha = rz / pq
        x = add_poly(x, alpha, p)
        if step == iters - 1:
            break
        z = add_poly(z, -alpha, q)
        rz_new = jnp.maximum(inner(z, z, moments), 1e-35)
        p = add_poly(z, rz_new / rz, p)
        rz = rz_new
    return x


def kernel(
    nlon, nlat,
    tr, uu, vv, surf, land, bot, w_in, b_in, w_mid, b_mid, w_out,
    tr_out, u_out, v_out, s_out,
    wet_s, msk_s, clo_s, X, U, V, D, zs, w1s, w2s,
    wbig, wmt, wob, bias1, bias2, h1, h2,
    pack_w, pack_e, row_n, row_s, recv_e, recv_w, recv_n, recv_s,
    red1, red2, halo_send, halo_recv, send1, recv1, send2, recv2,
):
    lev, rows, cols = tr.shape
    hid = w_mid.shape[0]
    lon, lat = lax.axis_index("lon"), lax.axis_index("lat")
    east, west = lax.rem(lon + 1, nlon), lax.rem(lon + nlon - 1, nlon)
    north, south = lax.rem(lat + 1, nlat), lax.rem(lat + nlat - 1, nlat)

    barrier = pltpu.get_barrier_semaphore()
    for d in range(1, nlon):
        pl.semaphore_signal(barrier, inc=1, device_id=(lax.rem(lon + d, nlon), lat), device_id_type=MESH)
    for d in range(1, nlat):
        pl.semaphore_signal(barrier, inc=1, device_id=(lon, lax.rem(lat + d, nlat)), device_id_type=MESH)
    for a in (east, west):
        for b in (north, south):
            pl.semaphore_signal(barrier, inc=1, device_id=(a, b), device_id_type=MESH)

    step = 8

    @pl.loop(0, rows // step)
    def _(g):
        r0 = pl.multiple_of(g * step, step)
        rs = pl.ds(r0, step)
        bottom = bot[rs, :]
        j = (lat * rows + r0 + lax.broadcasted_iota(jnp.int32, (step, 1), 0)).astype(F32)
        f = 2.0 * (j + 0.5) / (rows * nlat) - 1.0
        su = sv = sd = None
        for l in range(lev):
            wet = jnp.where(l < bottom, land[l, rs, :], 0).astype(F32)
            half_floor = jnp.where(bottom == l + 1, 0.5, 0.0)
            u, v = uu[l, rs, :], vv[l, rs, :]
            scaled = 0.2 * wet
            us = u + scaled * (f * v - half_floor * u)
            vs = v + scaled * (-f * u - half_floor * v)
            u_out[l, rs, :] = us
            v_out[l, rs, :] = vs
            wet_s[l, rs, :] = wet
            msk_s[l, rs, :] = wet * tr[l, rs, :]
            su = wet * us if su is None else su + wet * us
            sv = wet * vs if sv is None else sv + wet * vs
            sd = wet if sd is None else sd + wet
        U[rs, :cols] = su
        V[rs, :cols] = sv
        D[rs, :cols] = sd
        X[rs, :cols] = surf[rs, :]

    lane = lax.broadcasted_iota(jnp.int32, (rows, 128), 1)
    fields = (U, V, D, X)
    for pack, at, edge, width_at in ((pack_w, 0, 0, 0), (pack_e, cols - 128, 127, 128 - HALO)):
        acc = jnp.zeros((rows, 128), F32)
        for k, ref in enumerate(fields):
            moved = pltpu.roll(ref[:rows, at : at + 128], (HALO * k - width_at) % 128, 1)
            acc = jnp.where((lane >= HALO * k) & (lane < HALO * (k + 1)), moved, acc)
        for l in range(lev):
            for m, ref in enumerate((msk_s, wet_s)):
                to = HALO * 4 + m * lev + l
                moved = pltpu.roll(ref[l, :, at : at + 128], (to - edge) % 128, 1)
                acc = jnp.where(lane == to, moved, acc)
        pack[...] = acc
    for buf, at, edge in ((row_n, rows - 8, rows - 1), (row_s, 0, 0)):
        for k, ref in enumerate(fields):
            buf[8 * k : 8 * k + 8, :] = ref[at : at + 8, :cols]
        for l in range(lev):
            buf[32 + l : 33 + l, :] = msk_s[l, edge : edge + 1, :]
            buf[32 + lev + l : 33 + lev + l, :] = wet_s[l, edge : edge + 1, :]

    pl.semaphore_wait(barrier, nlon - 1 + nlat - 1 + 4)

    plan = (
        (pack_w, recv_e.at[pl.ds(0, rows)], (west, lat)),
        (pack_e, recv_w.at[pl.ds(0, rows)], (east, lat)),
        (row_n, recv_s, (lon, north)),
        (row_s, recv_n, (lon, south)),
        (pack_w.at[pl.ds(rows - 8, 8)], recv_e.at[pl.ds(rows + 8, 8)], (west, north)),
        (pack_e.at[pl.ds(rows - 8, 8)], recv_w.at[pl.ds(rows + 8, 8)], (east, north)),
        (pack_w.at[pl.ds(0, 8)], recv_e.at[pl.ds(rows, 8)], (west, south)),
        (pack_e.at[pl.ds(0, 8)], recv_w.at[pl.ds(rows, 8)], (east, south)),
    )
    halo_copies = []
    for i, (src, dst, dev) in enumerate(plan):
        halo_copies.append(pltpu.make_async_remote_copy(
            src_ref=src, dst_ref=dst, send_sem=halo_send.at[i], recv_sem=halo_recv.at[i],
            device_id=dev, device_id_type=MESH))
    for c in halo_copies:
        c.start()

    nf = w_in.shape[0]
    spread = (lax.broadcasted_iota(jnp.int32, (nf, nf * 8), 0)
              == lax.broadcasted_iota(jnp.int32, (nf, nf * 8), 1) // 8).astype(F32).astype(BF16)
    wide = lax.dot_general(w_in[...], spread, TN, preferred_element_type=F32)
    which = lax.broadcasted_iota(jnp.int32, wide.shape, 1) % 8
    for jj in range(8):
        wbig[jj * hid : (jj + 1) * hid, :] = jnp.where(which == jj, wide, 0.0).astype(BF16)
    eye = (lax.broadcasted_iota(jnp.int32, (hid, hid), 0)
           == lax.broadcasted_iota(jnp.int32, (hid, hid), 1))
    wmt[...] = lax.dot_general(w_mid[...], eye.astype(F32).astype(BF16), TN, preferred_element_type=F32).astype(BF16)
    pick = (lax.broadcasted_iota(jnp.int32, (lev * 8, lev), 0) // 8
            == lax.broadcasted_iota(jnp.int32, (lev * 8, lev), 1)).astype(F32).astype(BF16)
    tall = lax.dot_general(pick, w_out[...], NT, preferred_element_type=F32)
    which = lax.broadcasted_iota(jnp.int32, tall.shape, 0) % 8
    for jj in range(8):
        wob[:, jj * hid : (jj + 1) * hid] = jnp.where(which == jj, tall, 0.0).astype(BF16)
    for b, bias in ((b_in, bias1), (b_mid, bias2)):
        column = jnp.sum(jnp.where(eye, b[...], 0.0), axis=1, keepdims=True)
        bias[...] = jnp.broadcast_to(column, bias.shape)

    def network(g):
        rs = pl.ds(pl.multiple_of(g * 8, 8), 8)
        feats = jnp.concatenate(
            [ref[:, rs, :].reshape(lev * 8, cols) for ref in (tr, uu, vv)], axis=0).astype(BF16)
        for jj in range(8):
            at = slice(jj * hid, (jj + 1) * hid)
            first = jnp.dot(wbig[at, :], feats, preferred_element_type=F32)
            h1[at, :] = jnp.tanh(first + bias1[...]).astype(BF16)
        for jj in range(8):
            at = slice(jj * hid, (jj + 1) * hid)
            second = jnp.dot(wmt[...], h1[at, :], preferred_element_type=F32)
            h2[at, :] = jnp.tanh(second + bias2[...]).astype(BF16)
        out = jnp.dot(wob[...], h2[...], preferred_element_type=F32)
        clo_s[:, rs, :] = out.reshape(lev, 8, cols)

    groups = rows // 8
    cut1, cut2 = groups // 2, groups * 3 // 4
    pl.loop(0, cut1)(network)

    for c in halo_copies:
        c.wait_recv()

    open_n = jnp.where(lat == nlat - 1, 0.0, 1.0).astype(F32)
    open_s = jnp.where(lat == 0, 0.0, 1.0).astype(F32)
    ext_rows = rows + 16
    lane = lax.broadcasted_iota(jnp.int32, (ext_rows, 128), 1)
    row_id = lax.broadcasted_iota(jnp.int32, (ext_rows, 1), 0)
    inside = jnp.where(row_id < rows, 1.0, jnp.where(row_id < rows + 8, open_n, open_s))
    e_all, w_all = recv_e[...] * inside, recv_w[...] * inside
    for k, ref in enumerate(fields):
        side = jnp.where(lane < HALO, pltpu.roll(e_all, (-HALO * k) % 128, 1), 0.0)
        ref[:, cols:] = jnp.where(
            lane >= 128 - HALO, pltpu.roll(w_all, (128 - HALO - HALO * k) % 128, 1), side)
        ref[rows : rows + 8, :cols] = recv_n[8 * k : 8 * k + 8, :] * open_n
        ref[rows + 8 :, :cols] = recv_s[8 * k : 8 * k + 8, :] * open_s

    depth = D[...]
    face_e = jnp.minimum(depth, shift_to(depth, 1, 1))
    face_n = jnp.minimum(depth, shift_to(depth, 1, 0))
    face_w = shift_to(face_e, -1, 1)
    face_s = shift_to(face_n, -1, 0)
    precond = 1.0 + face_e + face_w + face_n + face_s
    inverse = 1.0 / precond

    def neighbours(x):
        return (face_e * shift_to(x, 1, 1) + face_w * shift_to(x, -1, 1)
                + face_n * shift_to(x, 1, 0) + face_s * shift_to(x, -1, 0))

    x0, ub, vb = X[...], U[...], V[...]
    div = 0.5 * (shift_to(ub, 1, 1) - shift_to(ub, -1, 1) + shift_to(vb, 1, 0) - shift_to(vb, -1, 0))
    resid = (x0 - div - precond * x0 + neighbours(x0)) * inside
    z0 = resid * inverse
    nz = neighbours(z0)
    w1 = nz * inverse
    nw1 = neighbours(w1)
    w2 = nw1 * inverse
    nw2 = neighbours(w2)
    zs[...] = z0
    w1s[...] = w1
    w2s[...] = w2
    pairs = ((z0, resid), (z0, nz), (w1, nz), (w1, nw1), (w2, nw1), (w2, nw2))
    parts = []
    for a, b in pairs:
        prod = a[:rows, :cols] * b[:rows, :cols]
        prod = prod[:, :128] + prod[:, 128:] if cols == 256 else sum(
            prod[:, c : c + 128] for c in range(0, cols, 128))
        parts.append(jnp.sum(prod, axis=0, keepdims=True))
    parts.append(jnp.zeros((8 - len(parts), 128), F32))
    red1[lon] = jnp.concatenate(parts, axis=0)

    def exchange(ref, send, recv, me, count, device):
        copies = []
        for d in range(1, count):
            target = lax.rem(me + d, count)
            copies.append(pltpu.make_async_remote_copy(
                src_ref=ref.at[me], dst_ref=ref.at[me], send_sem=send.at[d], recv_sem=recv.at[d],
                device_id=device(target), device_id_type=MESH))
        for c in copies:
            c.start()
        return copies

    def arrived(ref, send, recv, me, count, device):
        for d in range(1, count):
            source = lax.rem(me + count - d, count)
            pltpu.make_async_remote_copy(
                src_ref=ref.at[source], dst_ref=ref.at[source], send_sem=send.at[d], recv_sem=recv.at[d],
                device_id=device(source), device_id_type=MESH).wait_recv()

    along_lon = (red1, send1, recv1, lon, nlon, lambda t: (t, lat))
    along_lat = (red2, send2, recv2, lat, nlat, lambda t: (lon, t))
    copies1 = exchange(*along_lon)
    pl.loop(cut1, cut2)(network)
    arrived(*along_lon)
    red2[lat] = jnp.sum(red1[...], axis=0)
    copies2 = exchange(*along_lat)
    pl.loop(cut2, groups)(network)

    col_id = lax.broadcasted_iota(jnp.int32, (rows, cols), 1)
    line_id = lax.broadcasted_iota(jnp.int32, (rows, cols), 0)
    for l in range(lev):
        def around(ref, m):
            a = ref[l]
            to = HALO * 4 + m * lev + l
            at = 32 + m * lev + l
            e = jnp.where(col_id == cols - 1, recv_e[:rows, to : to + 1], shift_to(a, 1, 1))
            w = jnp.where(col_id == 0, recv_w[:rows, to : to + 1], shift_to(a, -1, 1))
            n = jnp.where(line_id == rows - 1, recv_n[at : at + 1, :] * open_n, shift_to(a, 1, 0))
            s = jnp.where(line_id == 0, recv_s[at : at + 1, :] * open_s, shift_to(a, -1, 0))
            return e, w, n, s

        e, w, n, s = around(msk_s, 0)
        we, ww, wn, ws = around(wet_s, 1)
        t = tr[l]
        lap = (e + w + n + s) - t * (we + ww + wn + ws)
        adv = -0.5 * (uu[l] * (e - w) + vv[l] * (n - s))
        tr_out[l] = t + 0.2 * wet_s[l] * (lap + adv + clo_s[l])

    arrived(*along_lat)
    total = jnp.sum(jnp.sum(red2[...], axis=0), axis=1, keepdims=True)
    moments = [total[k : k + 1, :] for k in range(6)]
    c = cg_coefficients(moments, 3, 1.0 + 4.0 * lev + 1.0)
    x = X[...] + c[0] * zs[...] + c[1] * w1s[...] + c[2] * w2s[...]
    s_out[...] = x[:rows, :cols]
    half_x = 0.5 * (shift_to(x, 1, 1) - shift_to(x, -1, 1))[:rows, :cols]
    half_y = 0.5 * (shift_to(x, 1, 0) - shift_to(x, -1, 0))[:rows, :cols]
    zs[:rows, :cols] = half_x
    w1s[:rows, :cols] = half_y

    @pl.loop(0, rows // step)
    def _(g):
        rs = pl.ds(pl.multiple_of(g * step, step), step)
        gx, gy = zs[rs, :cols], w1s[rs, :cols]
        for l in range(lev):
            wet = wet_s[l, rs, :]
            u_out[l, rs, :] = wet * (u_out[l, rs, :] - gx)
            v_out[l, rs, :] = wet * (v_out[l, rs, :] - gy)

    for c in halo_copies + copies1 + copies2:
        c.wait_send()


def on_device(nlon, nlat, tracer, u_vel, v_vel, surface, land_mask, bottom, w_in, b_in, w_mid, b_mid, w_out):
    lev, rows, cols = tracer.shape
    hid = w_mid.shape[0]
    ext = (rows + 16, cols + 128)
    cube = jax.ShapeDtypeStruct(tracer.shape, F32)
    vmem = pl.BlockSpec(memory_space=pltpu.VMEM)
    strip = 32 + 2 * lev
    scratch = (
        [pltpu.VMEM(tracer.shape, F32)] * 3
        + [pltpu.VMEM(ext, F32)] * 7
        + [
            pltpu.VMEM((8 * hid, 24 * lev), BF16),
            pltpu.VMEM((hid, hid), BF16),
            pltpu.VMEM((8 * lev, 8 * hid), BF16),
            pltpu.VMEM((hid, cols), F32),
            pltpu.VMEM((hid, cols), F32),
            pltpu.VMEM((8 * hid, cols), BF16),
            pltpu.VMEM((8 * hid, cols), BF16),
        ]
        + [pltpu.VMEM((rows, 128), F32)] * 2
        + [pltpu.VMEM((strip, cols), F32)] * 2
        + [pltpu.VMEM((rows + 16, 128), F32)] * 2
        + [pltpu.VMEM((strip, cols), F32)] * 2
        + [pltpu.VMEM((nlon, 8, 128), F32), pltpu.VMEM((nlat, 8, 128), F32)]
        + [pltpu.SemaphoreType.DMA((8,))] * 2
        + [pltpu.SemaphoreType.DMA((nlon,))] * 2
        + [pltpu.SemaphoreType.DMA((nlat,))] * 2
    )
    return pl.pallas_call(
        functools.partial(kernel, nlon, nlat),
        out_shape=(cube, cube, cube, jax.ShapeDtypeStruct(surface.shape, F32)),
        in_specs=[vmem] * 11,
        out_specs=(vmem,) * 4,
        scratch_shapes=scratch,
        compiler_params=pltpu.CompilerParams(
            collective_id=0, has_side_effects=True, vmem_limit_bytes=48 * 2**20),
    )(tracer, u_vel, v_vel, surface, land_mask, bottom, w_in, b_in[None], w_mid, b_mid[None], w_out)


def solution(mesh):
    cube, plane = P(None, "lat", "lon"), P("lat", "lon")
    return jax.shard_map(
        functools.partial(on_device, mesh.shape["lon"], mesh.shape["lat"]),
        mesh=mesh,
        in_specs=(cube, cube, cube, plane, cube, plane, P(), P(), P(), P(), P()),
        out_specs=(cube, cube, cube, plane),
        check_vma=False,
    )
```

```python
import functools

import jax
import jax.numpy as jnp
from jax import lax
from jax.experimental import pallas as pl
from jax.experimental.pallas import tpu as pltpu
from jax.sharding import PartitionSpec as P

MESH = pl.DeviceIdType.MESH
QUARTERS = 4
HALO = 4
F32 = jnp.float32
BF16 = jnp.bfloat16
TN = (((0,), (0,)), ((), ()))


def shift_to(x, offset, axis):
    return pltpu.roll(x, (-offset) % x.shape[axis], axis)


def inner(a, b, moments):
    out = None
    for i, ai in enumerate(a):
        for j, bj in enumerate(b):
            term = ai * bj * moments[i + j]
            out = term if out is None else out + term
    return out


def scaled_minus_shift(p):
    out = [p[0]]
    for lower, upper in zip(p[:-1], p[1:]):
        out.append(upper - lower)
    out.append(-p[-1])
    return out


def add_poly(a, scale, b):
    out = []
    for i in range(max(len(a), len(b))):
        if i >= len(a):
            out.append(scale * b[i])
        elif i >= len(b):
            out.append(a[i])
        else:
            out.append(a[i] + scale * b[i])
    return out


def cg_coefficients(moments, iters, top):
    one = jnp.ones_like(moments[0])
    z, p, x = [one], [one], [jnp.zeros_like(one)]
    rz = moments[0]
    for step in range(iters):
        q = scaled_minus_shift(p)
        pq = jnp.maximum(inner(p, q, moments), rz * (1.0 / top))
        alpha = rz / pq
        x = add_poly(x, alpha, p)
        if step == iters - 1:
            break
        z = add_poly(z, -alpha, q)
        rz_new = jnp.maximum(inner(z, z, moments), 1e-35)
        p = add_poly(z, rz_new / rz, p)
        rz = rz_new
    return x


def kernel(
    nlon, nlat,
    tr_h, uu_h, vv_h, surf_h, land_h, bot_h, w_in_h, b_in_h, w_mid_h, b_mid_h, w_out_h,
    tr_out, u_out, v_out, s_out, wet_s, gx_out, gy_out,
    tr, uu, vv, surf, land, bot, w_in, b_in, w_mid, b_mid, w_out,
    msk_s, clo_s, X, U, V, D, zs, w1s, w2s,
    wbig, wmt, wob, bias1, bias2, h1, h2,
    pack_w, pack_e, row_n, row_s, recv_e, recv_w, recv_n, recv_s,
    red1, red2, load_small, load_big, halo_send, halo_recv, send1, recv1, send2, recv2,
):
    lev, rows, cols = tr.shape
    hid = w_mid.shape[0]
    lon, lat = lax.axis_index("lon"), lax.axis_index("lat")
    east, west = lax.rem(lon + 1, nlon), lax.rem(lon + nlon - 1, nlon)
    north, south = lax.rem(lat + 1, nlat), lax.rem(lat + nlat - 1, nlat)

    small = []
    for i, (src, dst) in enumerate((
        (w_in_h, w_in), (w_mid_h, w_mid), (w_out_h, w_out), (b_in_h, b_in), (b_mid_h, b_mid),
        (bot_h, bot), (surf_h, surf),
    )):
        small.append(pltpu.make_async_copy(src, dst, load_small.at[i]))
    big = []
    for q in range(QUARTERS):
        part = pl.ds(q * (rows // QUARTERS), rows // QUARTERS)
        for i, (src, dst) in enumerate(((land_h, land), (uu_h, uu), (vv_h, vv), (tr_h, tr))):
            big.append(pltpu.make_async_copy(src.at[:, part], dst.at[:, part], load_big.at[4 * q + i]))
    for c in small + big:
        c.start()

    barrier = pltpu.get_barrier_semaphore()
    for d in range(1, nlon):
        pl.semaphore_signal(barrier, inc=1, device_id=(lax.rem(lon + d, nlon), lat), device_id_type=MESH)
    for d in range(1, nlat):
        pl.semaphore_signal(barrier, inc=1, device_id=(lon, lax.rem(lat + d, nlat)), device_id_type=MESH)
    for a in (east, west):
        for b in (north, south):
            pl.semaphore_signal(barrier, inc=1, device_id=(a, b), device_id_type=MESH)

    for c in small:
        c.wait()

    nf = w_in.shape[0]
    spread = (lax.broadcasted_iota(jnp.int32, (nf, nf * 8), 0)
              == lax.broadcasted_iota(jnp.int32, (nf, nf * 8), 1) // 8).astype(F32).astype(BF16)
    wide = lax.dot_general(w_in[...], spread, TN, preferred_element_type=F32)
    which = lax.broadcasted_iota(jnp.int32, wide.shape, 1) % 8
    for jj in range(8):
        wbig[jj * hid : (jj + 1) * hid, :] = jnp.where(which == jj, wide, 0.0).astype(BF16)
    eye = (lax.broadcasted_iota(jnp.int32, (hid, hid), 0)
           == lax.broadcasted_iota(jnp.int32, (hid, hid), 1))
    wmt[...] = lax.dot_general(w_mid[...], eye.astype(F32).astype(BF16), TN, preferred_element_type=F32).astype(BF16)
    pick = (lax.broadcasted_iota(jnp.int32, (lev * 8, lev), 0) // 8
            == lax.broadcasted_iota(jnp.int32, (lev * 8, lev), 1)).astype(F32).astype(BF16)
    tall = jnp.dot(pick, w_out[...], preferred_element_type=F32)
    which = lax.broadcasted_iota(jnp.int32, tall.shape, 0) % 8
    for jj in range(8):
        wob[:, jj * hid : (jj + 1) * hid] = jnp.where(which == jj, tall, 0.0).astype(BF16)
    for b, bias in ((b_in, bias1), (b_mid, bias2)):
        column = jnp.sum(jnp.where(eye, b[...], 0.0), axis=1, keepdims=True)
        bias[...] = jnp.broadcast_to(column, bias.shape)

    step = 8

    def momentum(g):
        r0 = pl.multiple_of(g * step, step)
        rs = pl.ds(r0, step)
        bottom = bot[rs, :]
        j = (lat * rows + r0 + lax.broadcasted_iota(jnp.int32, (step, 1), 0)).astype(F32)
        f = 2.0 * (j + 0.5) / (rows * nlat) - 1.0
        su = sv = sd = None
        for l in range(lev):
            wet = jnp.where(l < bottom, land[l, rs, :], 0).astype(F32)
            half_floor = jnp.where(bottom == l + 1, 0.5, 0.0)
            u, v = uu[l, rs, :], vv[l, rs, :]
            scaled = 0.2 * wet
            us = u + scaled * (f * v - half_floor * u)
            vs = v + scaled * (-f * u - half_floor * v)
            u_out[l, rs, :] = us
            v_out[l, rs, :] = vs
            wet_s[l, rs, :] = wet
            msk_s[l, rs, :] = wet * tr[l, rs, :]
            su = wet * us if su is None else su + wet * us
            sv = wet * vs if sv is None else sv + wet * vs
            sd = wet if sd is None else sd + wet
        U[rs, :cols] = su
        V[rs, :cols] = sv
        D[rs, :cols] = sd
        X[rs, :cols] = surf[rs, :]

    for q in range(QUARTERS):
        for c in big[4 * q : 4 * q + 4]:
            c.wait()
        per = rows // step // QUARTERS
        pl.loop(q * per, (q + 1) * per)(momentum)

    lane = lax.broadcasted_iota(jnp.int32, (rows, 128), 1)
    fields = (U, V, D, X)
    for pack, at, edge, width_at in ((pack_w, 0, 0, 0), (pack_e, cols - 128, 127, 128 - HALO)):
        acc = jnp.zeros((rows, 128), F32)
        for k, ref in enumerate(fields):
            moved = pltpu.roll(ref[:rows, at : at + 128], (HALO * k - width_at) % 128, 1)
            acc = jnp.where((lane >= HALO * k) & (lane < HALO * (k + 1)), moved, acc)
        for l in range(lev):
            for m, ref in enumerate((msk_s, wet_s)):
                to = HALO * 4 + m * lev + l
                moved = pltpu.roll(ref[l, :, at : at + 128], (to - edge) % 128, 1)
                acc = jnp.where(lane == to, moved, acc)
        pack[...] = acc
    for buf, at, edge in ((row_n, rows - 8, rows - 1), (row_s, 0, 0)):
        for k, ref in enumerate(fields):
            buf[8 * k : 8 * k + 8, :] = ref[at : at + 8, :cols]
        for l in range(lev):
            buf[32 + l : 33 + l, :] = msk_s[l, edge : edge + 1, :]
            buf[32 + lev + l : 33 + lev + l, :] = wet_s[l, edge : edge + 1, :]

    pl.semaphore_wait(barrier, nlon - 1 + nlat - 1 + 4)

    plan = (
        (pack_w, recv_e.at[pl.ds(0, rows)], (west, lat)),
        (pack_e, recv_w.at[pl.ds(0, rows)], (east, lat)),
        (row_n, recv_s, (lon, north)),
        (row_s, recv_n, (lon, south)),
        (pack_w.at[pl.ds(rows - 8, 8)], recv_e.at[pl.ds(rows + 8, 8)], (west, north)),
        (pack_e.at[pl.ds(rows - 8, 8)], recv_w.at[pl.ds(rows + 8, 8)], (east, north)),
        (pack_w.at[pl.ds(0, 8)], recv_e.at[pl.ds(rows, 8)], (west, south)),
        (pack_e.at[pl.ds(0, 8)], recv_w.at[pl.ds(rows, 8)], (east, south)),
    )
    halo_copies = []
    for i, (src, dst, dev) in enumerate(plan):
        halo_copies.append(pltpu.make_async_remote_copy(
            src_ref=src, dst_ref=dst, send_sem=halo_send.at[i], recv_sem=halo_recv.at[i],
            device_id=dev, device_id_type=MESH))
    for c in halo_copies:
        c.start()

    def network(g):
        rs = pl.ds(pl.multiple_of(g * 8, 8), 8)
        feats = jnp.concatenate(
            [ref[:, rs, :].reshape(lev * 8, cols) for ref in (tr, uu, vv)], axis=0).astype(BF16)
        for jj in range(8):
            at = slice(jj * hid, (jj + 1) * hid)
            first = jnp.dot(wbig[at, :], feats, preferred_element_type=F32)
            h1[at, :] = jnp.tanh(first + bias1[...]).astype(BF16)
        for jj in range(8):
            at = slice(jj * hid, (jj + 1) * hid)
            second = jnp.dot(wmt[...], h1[at, :], preferred_element_type=F32)
            h2[at, :] = jnp.tanh(second + bias2[...]).astype(BF16)
        out = jnp.dot(wob[...], h2[...], preferred_element_type=F32)
        clo_s[:, rs, :] = out.reshape(lev, 8, cols)

    groups = rows // 8
    cut1, cut2 = groups // 2, groups * 3 // 4
    pl.loop(0, cut1)(network)

    for c in halo_copies:
        c.wait_recv()

    open_n = jnp.where(lat == nlat - 1, 0.0, 1.0).astype(F32)
    open_s = jnp.where(lat == 0, 0.0, 1.0).astype(F32)
    ext_rows = rows + 16
    lane = lax.broadcasted_iota(jnp.int32, (ext_rows, 128), 1)
    row_id = lax.broadcasted_iota(jnp.int32, (ext_rows, 1), 0)
    inside = jnp.where(row_id < rows, 1.0, jnp.where(row_id < rows + 8, open_n, open_s))
    e_all, w_all = recv_e[...] * inside, recv_w[...] * inside
    for k, ref in enumerate(fields):
        side = jnp.where(lane < HALO, pltpu.roll(e_all, (-HALO * k) % 128, 1), 0.0)
        ref[:, cols:] = jnp.where(
            lane >= 128 - HALO, pltpu.roll(w_all, (128 - HALO - HALO * k) % 128, 1), side)
        ref[rows : rows + 8, :cols] = recv_n[8 * k : 8 * k + 8, :] * open_n
        ref[rows + 8 :, :cols] = recv_s[8 * k : 8 * k + 8, :] * open_s

    depth = D[...]
    face_e = jnp.minimum(depth, shift_to(depth, 1, 1))
    face_n = jnp.minimum(depth, shift_to(depth, 1, 0))
    face_w = shift_to(face_e, -1, 1)
    face_s = shift_to(face_n, -1, 0)
    precond = 1.0 + face_e + face_w + face_n + face_s
    inverse = 1.0 / precond

    def neighbours(x):
        return (face_e * shift_to(x, 1, 1) + face_w * shift_to(x, -1, 1)
                + face_n * shift_to(x, 1, 0) + face_s * shift_to(x, -1, 0))

    x0, ub, vb = X[...], U[...], V[...]
    div = 0.5 * (shift_to(ub, 1, 1) - shift_to(ub, -1, 1) + shift_to(vb, 1, 0) - shift_to(vb, -1, 0))
    resid = (x0 - div - precond * x0 + neighbours(x0)) * inside
    z0 = resid * inverse
    nz = neighbours(z0)
    w1 = nz * inverse
    nw1 = neighbours(w1)
    w2 = nw1 * inverse
    nw2 = neighbours(w2)
    zs[...] = z0
    w1s[...] = w1
    w2s[...] = w2
    pairs = ((z0, resid), (z0, nz), (w1, nz), (w1, nw1), (w2, nw1), (w2, nw2))
    parts = []
    for a, b in pairs:
        prod = a[:rows, :cols] * b[:rows, :cols]
        prod = prod[:, :128] + prod[:, 128:] if cols == 256 else sum(
            prod[:, c : c + 128] for c in range(0, cols, 128))
        parts.append(jnp.sum(prod, axis=0, keepdims=True))
    parts.append(jnp.zeros((8 - len(parts), 128), F32))
    red1[lon] = jnp.concatenate(parts, axis=0)

    def exchange(ref, send, recv, me, count, device):
        copies = []
        for d in range(1, count):
            target = lax.rem(me + d, count)
            copies.append(pltpu.make_async_remote_copy(
                src_ref=ref.at[me], dst_ref=ref.at[me], send_sem=send.at[d], recv_sem=recv.at[d],
                device_id=device(target), device_id_type=MESH))
        for c in copies:
            c.start()
        return copies

    def arrived(ref, send, recv, me, count, device):
        for d in range(1, count):
            source = lax.rem(me + count - d, count)
            pltpu.make_async_remote_copy(
                src_ref=ref.at[source], dst_ref=ref.at[source], send_sem=send.at[d], recv_sem=recv.at[d],
                device_id=device(source), device_id_type=MESH).wait_recv()

    along_lon = (red1, send1, recv1, lon, nlon, lambda t: (t, lat))
    along_lat = (red2, send2, recv2, lat, nlat, lambda t: (lon, t))
    copies1 = exchange(*along_lon)
    pl.loop(cut1, cut2)(network)
    arrived(*along_lon)
    red2[lat] = jnp.sum(red1[...], axis=0)
    copies2 = exchange(*along_lat)
    pl.loop(cut2, groups)(network)

    col_id = lax.broadcasted_iota(jnp.int32, (rows, cols), 1)
    line_id = lax.broadcasted_iota(jnp.int32, (rows, cols), 0)
    for l in range(lev):
        def around(ref, m):
            a = ref[l]
            to = HALO * 4 + m * lev + l
            at = 32 + m * lev + l
            e = jnp.where(col_id == cols - 1, recv_e[:rows, to : to + 1], shift_to(a, 1, 1))
            w = jnp.where(col_id == 0, recv_w[:rows, to : to + 1], shift_to(a, -1, 1))
            n = jnp.where(line_id == rows - 1, recv_n[at : at + 1, :] * open_n, shift_to(a, 1, 0))
            s = jnp.where(line_id == 0, recv_s[at : at + 1, :] * open_s, shift_to(a, -1, 0))
            return e, w, n, s

        e, w, n, s = around(msk_s, 0)
        we, ww, wn, ws = around(wet_s, 1)
        t = tr[l]
        lap = (e + w + n + s) - t * (we + ww + wn + ws)
        adv = -0.5 * (uu[l] * (e - w) + vv[l] * (n - s))
        tr_out[l] = t + 0.2 * wet_s[l] * (lap + adv + clo_s[l])

    arrived(*along_lat)
    total = jnp.sum(jnp.sum(red2[...], axis=0), axis=1, keepdims=True)
    moments = [total[k : k + 1, :] for k in range(6)]
    c = cg_coefficients(moments, 3, 1.0 + 4.0 * lev + 1.0)
    x = X[...] + c[0] * zs[...] + c[1] * w1s[...] + c[2] * w2s[...]
    s_out[...] = x[:rows, :cols]
    gx_out[...] = 0.5 * (shift_to(x, 1, 1) - shift_to(x, -1, 1))[:rows, :cols]
    gy_out[...] = 0.5 * (shift_to(x, 1, 0) - shift_to(x, -1, 0))[:rows, :cols]

    for c in halo_copies + copies1 + copies2:
        c.wait_send()


def finish(tr, us, vs, surf, wet, gx, gy, tr_h, u_h, v_h, s_h, u, v, whole_sem, part_sem):
    lev, rows, cols = wet.shape
    copies = [
        pltpu.make_async_copy(tr, tr_h, whole_sem.at[0]),
        pltpu.make_async_copy(surf, s_h, whole_sem.at[1]),
    ]
    for c in copies:
        c.start()
    per = rows // QUARTERS
    for q in range(QUARTERS):

        @pl.loop(0, per // 8)
        def _(g):
            rs = pl.ds(pl.multiple_of(q * per + g * 8, 8), 8)
            x, y = gx[rs, :], gy[rs, :]
            for l in range(lev):
                w = wet[l, rs, :]
                u[l, rs, :] = w * (us[l, rs, :] - x)
                v[l, rs, :] = w * (vs[l, rs, :] - y)

        part = pl.ds(q * per, per)
        for i, (src, dst) in enumerate(((u, u_h), (v, v_h))):
            c = pltpu.make_async_copy(src.at[:, part], dst.at[:, part], part_sem.at[2 * q + i])
            c.start()
            copies.append(c)
    for c in copies:
        c.wait()


def on_device(nlon, nlat, tracer, u_vel, v_vel, surface, land_mask, bottom, w_in, b_in, w_mid, b_mid, w_out):
    lev, rows, cols = tracer.shape
    hid = w_mid.shape[0]
    ext = (rows + 16, cols + 128)
    cube = jax.ShapeDtypeStruct(tracer.shape, F32)
    vmem = pl.BlockSpec(memory_space=pltpu.VMEM)
    args = (tracer, u_vel, v_vel, surface, land_mask, bottom, w_in, b_in[None], w_mid, b_mid[None], w_out.T)
    plane = jax.ShapeDtypeStruct(surface.shape, F32)
    hbm = pl.BlockSpec(memory_space=pltpu.HBM)
    strip = 32 + 2 * lev
    scratch = (
        [pltpu.VMEM(a.shape, a.dtype) for a in args]
        + [pltpu.VMEM(tracer.shape, F32)] * 2
        + [pltpu.VMEM(ext, F32)] * 7
        + [
            pltpu.VMEM((8 * hid, 24 * lev), BF16),
            pltpu.VMEM((hid, hid), BF16),
            pltpu.VMEM((8 * lev, 8 * hid), BF16),
            pltpu.VMEM((hid, cols), F32),
            pltpu.VMEM((hid, cols), F32),
            pltpu.VMEM((8 * hid, cols), BF16),
            pltpu.VMEM((8 * hid, cols), BF16),
        ]
        + [pltpu.VMEM((rows, 128), F32)] * 2
        + [pltpu.VMEM((strip, cols), F32)] * 2
        + [pltpu.VMEM((rows + 16, 128), F32)] * 2
        + [pltpu.VMEM((strip, cols), F32)] * 2
        + [pltpu.VMEM((nlon, 8, 128), F32), pltpu.VMEM((nlat, 8, 128), F32)]
        + [pltpu.SemaphoreType.DMA((7,)), pltpu.SemaphoreType.DMA((4 * QUARTERS,))]
        + [pltpu.SemaphoreType.DMA((8,))] * 2
        + [pltpu.SemaphoreType.DMA((nlon,))] * 2
        + [pltpu.SemaphoreType.DMA((nlat,))] * 2
    )
    held = pl.pallas_call(
        functools.partial(kernel, nlon, nlat),
        out_shape=(cube, cube, cube, plane, cube, plane, plane),
        in_specs=[hbm] * 11,
        out_specs=(vmem,) * 7,
        scratch_shapes=scratch,
        compiler_params=pltpu.CompilerParams(
            collective_id=0, has_side_effects=True, vmem_limit_bytes=40 * 2**20),
    )(*[pltpu.with_memory_space_constraint(a, pltpu.HBM) for a in args])
    return pl.pallas_call(
        finish,
        out_shape=(cube, cube, cube, plane),
        in_specs=[vmem] * 7,
        out_specs=(hbm,) * 4,
        scratch_shapes=[pltpu.VMEM(tracer.shape, F32)] * 2
        + [pltpu.SemaphoreType.DMA((2,)), pltpu.SemaphoreType.DMA((2 * QUARTERS,))],
        compiler_params=pltpu.CompilerParams(vmem_limit_bytes=40 * 2**20),
    )(*held)


def solution(mesh):
    cube, plane = P(None, "lat", "lon"), P("lat", "lon")
    return jax.shard_map(
        functools.partial(on_device, mesh.shape["lon"], mesh.shape["lat"]),
        mesh=mesh,
        in_specs=(cube, cube, cube, plane, cube, plane, P(), P(), P(), P(), P()),
        out_specs=(cube, cube, cube, plane),
        check_vma=False,
    )
```

```python
import functools

import jax
import jax.numpy as jnp
from jax import lax
from jax.experimental import pallas as pl
from jax.experimental.pallas import tpu as pltpu
from jax.sharding import PartitionSpec as P

MESH = pl.DeviceIdType.MESH
QUARTERS = 4
HALO = 4
F32 = jnp.float32
BF16 = jnp.bfloat16
TN = (((0,), (0,)), ((), ()))


def shift_to(x, offset, axis):
    return pltpu.roll(x, (-offset) % x.shape[axis], axis)


def inner(a, b, moments):
    out = None
    for i, ai in enumerate(a):
        for j, bj in enumerate(b):
            term = ai * bj * moments[i + j]
            out = term if out is None else out + term
    return out


def scaled_minus_shift(p):
    out = [p[0]]
    for lower, upper in zip(p[:-1], p[1:]):
        out.append(upper - lower)
    out.append(-p[-1])
    return out


def add_poly(a, scale, b):
    out = []
    for i in range(max(len(a), len(b))):
        if i >= len(a):
            out.append(scale * b[i])
        elif i >= len(b):
            out.append(a[i])
        else:
            out.append(a[i] + scale * b[i])
    return out


def cg_coefficients(moments, iters, top):
    one = jnp.ones_like(moments[0])
    z, p, x = [one], [one], [jnp.zeros_like(one)]
    rz = moments[0]
    for step in range(iters):
        q = scaled_minus_shift(p)
        pq = jnp.maximum(inner(p, q, moments), rz * (1.0 / top))
        alpha = rz / pq
        x = add_poly(x, alpha, p)
        if step == iters - 1:
            break
        z = add_poly(z, -alpha, q)
        rz_new = jnp.maximum(inner(z, z, moments), 1e-35)
        p = add_poly(z, rz_new / rz, p)
        rz = rz_new
    return x


def kernel(
    nlon, nlat,
    tr_h, uu_h, vv_h, surf_h, land_h, bot_h, w_in_h, b_in_h, w_mid_h, b_mid_h, w_out_h,
    tr_out, u_out, v_out, s_out, wet_s, gx_out, gy_out,
    tr, uu, vv, surf, land, bot, w_in, b_in, w_mid, b_mid, w_out,
    msk_s, clo_s, X, U, V, D, zs, w1s, w2s,
    wbig, wmt, wob, bias1, bias2, h1, h2,
    pack_w, pack_e, row_n, row_s, recv_e, recv_w, recv_n, recv_s,
    red1, load_small, load_big, halo_send, halo_recv, send1, recv1,
):
    lev, rows, cols = tr.shape
    hid = w_mid.shape[0]
    lon, lat = lax.axis_index("lon"), lax.axis_index("lat")
    east, west = lax.rem(lon + 1, nlon), lax.rem(lon + nlon - 1, nlon)
    north, south = lax.rem(lat + 1, nlat), lax.rem(lat + nlat - 1, nlat)

    small = []
    for i, (src, dst) in enumerate((
        (w_in_h, w_in), (w_mid_h, w_mid), (w_out_h, w_out), (b_in_h, b_in), (b_mid_h, b_mid),
        (bot_h, bot), (surf_h, surf),
    )):
        small.append(pltpu.make_async_copy(src, dst, load_small.at[i]))
    big = []
    for q in range(QUARTERS):
        part = pl.ds(q * (rows // QUARTERS), rows // QUARTERS)
        for i, (src, dst) in enumerate(((land_h, land), (uu_h, uu), (vv_h, vv), (tr_h, tr))):
            big.append(pltpu.make_async_copy(src.at[:, part], dst.at[:, part], load_big.at[4 * q + i]))
    for c in small + big:
        c.start()

    barrier = pltpu.get_barrier_semaphore()
    me, count = lon * nlat + lat, nlon * nlat
    for d in range(1, count):
        t = lax.rem(me + d, count)
        pl.semaphore_signal(barrier, inc=1, device_id=(t // nlat, lax.rem(t, nlat)), device_id_type=MESH)

    for c in small:
        c.wait()

    nf = w_in.shape[0]
    spread = (lax.broadcasted_iota(jnp.int32, (nf, nf * 8), 0)
              == lax.broadcasted_iota(jnp.int32, (nf, nf * 8), 1) // 8).astype(F32).astype(BF16)
    wide = lax.dot_general(w_in[...], spread, TN, preferred_element_type=F32)
    which = lax.broadcasted_iota(jnp.int32, wide.shape, 1) % 8
    for jj in range(8):
        wbig[jj * hid : (jj + 1) * hid, :] = jnp.where(which == jj, wide, 0.0).astype(BF16)
    eye = (lax.broadcasted_iota(jnp.int32, (hid, hid), 0)
           == lax.broadcasted_iota(jnp.int32, (hid, hid), 1))
    wmt[...] = lax.dot_general(w_mid[...], eye.astype(F32).astype(BF16), TN, preferred_element_type=F32).astype(BF16)
    pick = (lax.broadcasted_iota(jnp.int32, (lev * 8, lev), 0) // 8
            == lax.broadcasted_iota(jnp.int32, (lev * 8, lev), 1)).astype(F32).astype(BF16)
    tall = jnp.dot(pick, w_out[...], preferred_element_type=F32)
    which = lax.broadcasted_iota(jnp.int32, tall.shape, 0) % 8
    for jj in range(8):
        wob[:, jj * hid : (jj + 1) * hid] = jnp.where(which == jj, tall, 0.0).astype(BF16)
    for b, bias in ((b_in, bias1), (b_mid, bias2)):
        column = jnp.sum(jnp.where(eye, b[...], 0.0), axis=1, keepdims=True)
        bias[...] = jnp.broadcast_to(column, bias.shape)

    step = 8

    def momentum(g):
        r0 = pl.multiple_of(g * step, step)
        rs = pl.ds(r0, step)
        bottom = bot[rs, :]
        j = (lat * rows + r0 + lax.broadcasted_iota(jnp.int32, (step, 1), 0)).astype(F32)
        f = 2.0 * (j + 0.5) / (rows * nlat) - 1.0
        su = sv = sd = None
        for l in range(lev):
            wet = jnp.where(l < bottom, land[l, rs, :], 0).astype(F32)
            half_floor = jnp.where(bottom == l + 1, 0.5, 0.0)
            u, v = uu[l, rs, :], vv[l, rs, :]
            scaled = 0.2 * wet
            us = u + scaled * (f * v - half_floor * u)
            vs = v + scaled * (-f * u - half_floor * v)
            u_out[l, rs, :] = us
            v_out[l, rs, :] = vs
            wet_s[l, rs, :] = wet
            msk_s[l, rs, :] = wet * tr[l, rs, :]
            su = wet * us if su is None else su + wet * us
            sv = wet * vs if sv is None else sv + wet * vs
            sd = wet if sd is None else sd + wet
        U[rs, :cols] = su
        V[rs, :cols] = sv
        D[rs, :cols] = sd
        X[rs, :cols] = surf[rs, :]

    for q in range(QUARTERS):
        for c in big[4 * q : 4 * q + 4]:
            c.wait()
        per = rows // step // QUARTERS
        pl.loop(q * per, (q + 1) * per)(momentum)

    lane = lax.broadcasted_iota(jnp.int32, (rows, 128), 1)
    fields = (U, V, D, X)
    for pack, at, edge, width_at in ((pack_w, 0, 0, 0), (pack_e, cols - 128, 127, 128 - HALO)):
        acc = jnp.zeros((rows, 128), F32)
        for k, ref in enumerate(fields):
            moved = pltpu.roll(ref[:rows, at : at + 128], (HALO * k - width_at) % 128, 1)
            acc = jnp.where((lane >= HALO * k) & (lane < HALO * (k + 1)), moved, acc)
        for l in range(lev):
            for m, ref in enumerate((msk_s, wet_s)):
                to = HALO * 4 + m * lev + l
                moved = pltpu.roll(ref[l, :, at : at + 128], (to - edge) % 128, 1)
                acc = jnp.where(lane == to, moved, acc)
        pack[...] = acc
    for buf, at, edge in ((row_n, rows - 8, rows - 1), (row_s, 0, 0)):
        for k, ref in enumerate(fields):
            buf[8 * k : 8 * k + 8, :] = ref[at : at + 8, :cols]
        for l in range(lev):
            buf[32 + l : 33 + l, :] = msk_s[l, edge : edge + 1, :]
            buf[32 + lev + l : 33 + lev + l, :] = wet_s[l, edge : edge + 1, :]

    pl.semaphore_wait(barrier, count - 1)

    plan = (
        (pack_w, recv_e.at[pl.ds(0, rows)], (west, lat)),
        (pack_e, recv_w.at[pl.ds(0, rows)], (east, lat)),
        (row_n, recv_s, (lon, north)),
        (row_s, recv_n, (lon, south)),
        (pack_w.at[pl.ds(rows - 8, 8)], recv_e.at[pl.ds(rows + 8, 8)], (west, north)),
        (pack_e.at[pl.ds(rows - 8, 8)], recv_w.at[pl.ds(rows + 8, 8)], (east, north)),
        (pack_w.at[pl.ds(0, 8)], recv_e.at[pl.ds(rows, 8)], (west, south)),
        (pack_e.at[pl.ds(0, 8)], recv_w.at[pl.ds(rows, 8)], (east, south)),
    )
    halo_copies = []
    for i, (src, dst, dev) in enumerate(plan):
        halo_copies.append(pltpu.make_async_remote_copy(
            src_ref=src, dst_ref=dst, send_sem=halo_send.at[i], recv_sem=halo_recv.at[i],
            device_id=dev, device_id_type=MESH))
    has_north, has_south = lat < nlat - 1, lat > 0
    sent_if = (None, None, has_north, has_south, has_north, has_north, has_south, has_south)
    come_if = (None, None, has_south, has_north, has_south, has_south, has_north, has_north)

    def each(conditions, act):
        for c, condition in zip(halo_copies, conditions):
            if condition is None:
                act(c)
            else:
                pl.when(condition)(functools.partial(act, c))

    each(sent_if, lambda c: c.start())

    @pl.when(lat == nlat - 1)
    def _():
        recv_n[...] = jnp.zeros_like(recv_n)
        for ref in (recv_e, recv_w):
            ref[rows : rows + 8, :] = jnp.zeros((8, 128), F32)

    @pl.when(lat == 0)
    def _():
        recv_s[...] = jnp.zeros_like(recv_s)
        for ref in (recv_e, recv_w):
            ref[rows + 8 :, :] = jnp.zeros((8, 128), F32)

    def network(g):
        rs = pl.ds(pl.multiple_of(g * 8, 8), 8)
        feats = jnp.concatenate(
            [ref[:, rs, :].reshape(lev * 8, cols) for ref in (tr, uu, vv)], axis=0).astype(BF16)
        for jj in range(8):
            at = slice(jj * hid, (jj + 1) * hid)
            first = jnp.dot(wbig[at, :], feats, preferred_element_type=F32)
            h1[at, :] = jnp.tanh(first + bias1[...]).astype(BF16)
        for jj in range(8):
            at = slice(jj * hid, (jj + 1) * hid)
            second = jnp.dot(wmt[...], h1[at, :], preferred_element_type=F32)
            h2[at, :] = jnp.tanh(second + bias2[...]).astype(BF16)
        out = jnp.dot(wob[...], h2[...], preferred_element_type=F32)
        clo_s[:, rs, :] = out.reshape(lev, 8, cols)

    groups = rows // 8
    cut1 = groups // 2
    pl.loop(0, cut1, unroll=4)(network)

    each(come_if, lambda c: c.wait_recv())

    open_n = jnp.where(lat == nlat - 1, 0.0, 1.0).astype(F32)
    open_s = jnp.where(lat == 0, 0.0, 1.0).astype(F32)
    ext_rows = rows + 16
    lane = lax.broadcasted_iota(jnp.int32, (ext_rows, 128), 1)
    row_id = lax.broadcasted_iota(jnp.int32, (ext_rows, 1), 0)
    inside = jnp.where(row_id < rows, 1.0, jnp.where(row_id < rows + 8, open_n, open_s))
    e_all, w_all = recv_e[...] * inside, recv_w[...] * inside
    for k, ref in enumerate(fields):
        side = jnp.where(lane < HALO, pltpu.roll(e_all, (-HALO * k) % 128, 1), 0.0)
        ref[:, cols:] = jnp.where(
            lane >= 128 - HALO, pltpu.roll(w_all, (128 - HALO - HALO * k) % 128, 1), side)
        ref[rows : rows + 8, :cols] = recv_n[8 * k : 8 * k + 8, :] * open_n
        ref[rows + 8 :, :cols] = recv_s[8 * k : 8 * k + 8, :] * open_s

    depth = D[...]
    face_e = jnp.minimum(depth, shift_to(depth, 1, 1))
    face_n = jnp.minimum(depth, shift_to(depth, 1, 0))
    face_w = shift_to(face_e, -1, 1)
    face_s = shift_to(face_n, -1, 0)
    precond = 1.0 + face_e + face_w + face_n + face_s
    inverse = 1.0 / precond

    def neighbours(x):
        return (face_e * shift_to(x, 1, 1) + face_w * shift_to(x, -1, 1)
                + face_n * shift_to(x, 1, 0) + face_s * shift_to(x, -1, 0))

    x0, ub, vb = X[...], U[...], V[...]
    div = 0.5 * (shift_to(ub, 1, 1) - shift_to(ub, -1, 1) + shift_to(vb, 1, 0) - shift_to(vb, -1, 0))
    resid = (x0 - div - precond * x0 + neighbours(x0)) * inside
    z0 = resid * inverse
    nz = neighbours(z0)
    w1 = nz * inverse
    nw1 = neighbours(w1)
    w2 = nw1 * inverse
    nw2 = neighbours(w2)
    zs[...] = z0
    w1s[...] = w1
    w2s[...] = w2
    pairs = ((z0, resid), (z0, nz), (w1, nz), (w1, nw1), (w2, nw1), (w2, nw2))
    parts = []
    for a, b in pairs:
        prod = a[:rows, :cols] * b[:rows, :cols]
        prod = prod[:, :128] + prod[:, 128:] if cols == 256 else sum(
            prod[:, c : c + 128] for c in range(0, cols, 128))
        parts.append(jnp.sum(prod, axis=0, keepdims=True))
    parts.append(jnp.zeros((8 - len(parts), 128), F32))
    red1[me] = jnp.concatenate(parts, axis=0)

    def exchange(ref, send, recv, me, count, device):
        copies = []
        for d in range(1, count):
            target = lax.rem(me + d, count)
            copies.append(pltpu.make_async_remote_copy(
                src_ref=ref.at[me], dst_ref=ref.at[me], send_sem=send.at[d], recv_sem=recv.at[d],
                device_id=device(target), device_id_type=MESH))
        for c in copies:
            c.start()
        return copies

    def arrived(ref, send, recv, me, count, device):
        for d in range(1, count):
            source = lax.rem(me + count - d, count)
            pltpu.make_async_remote_copy(
                src_ref=ref.at[source], dst_ref=ref.at[source], send_sem=send.at[d], recv_sem=recv.at[d],
                device_id=device(source), device_id_type=MESH).wait_recv()

    everyone = (red1, send1, recv1, me, count, lambda t: (t // nlat, lax.rem(t, nlat)))
    copies1 = exchange(*everyone)
    pl.loop(cut1, groups, unroll=4)(network)

    col_id = lax.broadcasted_iota(jnp.int32, (rows, cols), 1)
    line_id = lax.broadcasted_iota(jnp.int32, (rows, cols), 0)
    for l in range(lev):
        def around(ref, m):
            a = ref[l]
            to = HALO * 4 + m * lev + l
            at = 32 + m * lev + l
            e = jnp.where(col_id == cols - 1, recv_e[:rows, to : to + 1], shift_to(a, 1, 1))
            w = jnp.where(col_id == 0, recv_w[:rows, to : to + 1], shift_to(a, -1, 1))
            n = jnp.where(line_id == rows - 1, recv_n[at : at + 1, :] * open_n, shift_to(a, 1, 0))
            s = jnp.where(line_id == 0, recv_s[at : at + 1, :] * open_s, shift_to(a, -1, 0))
            return e, w, n, s

        e, w, n, s = around(msk_s, 0)
        we, ww, wn, ws = around(wet_s, 1)
        t = tr[l]
        lap = (e + w + n + s) - t * (we + ww + wn + ws)
        adv = -0.5 * (uu[l] * (e - w) + vv[l] * (n - s))
        tr_out[l] = t + 0.2 * wet_s[l] * (lap + adv + clo_s[l])

    arrived(*everyone)
    total = jnp.sum(jnp.sum(red1[...], axis=0), axis=1, keepdims=True)
    moments = [total[k : k + 1, :] for k in range(6)]
    c = cg_coefficients(moments, 3, 1.0 + 4.0 * lev + 1.0)
    x = X[...] + c[0] * zs[...] + c[1] * w1s[...] + c[2] * w2s[...]
    s_out[...] = x[:rows, :cols]
    gx_out[...] = 0.5 * (shift_to(x, 1, 1) - shift_to(x, -1, 1))[:rows, :cols]
    gy_out[...] = 0.5 * (shift_to(x, 1, 0) - shift_to(x, -1, 0))[:rows, :cols]

    each(sent_if, lambda c: c.wait_send())
    for c in copies1:
        c.wait_send()


def finish(tr, us, vs, surf, wet, gx, gy, tr_h, u_h, v_h, s_h, u, v, whole_sem, part_sem):
    lev, rows, cols = wet.shape
    copies = [
        pltpu.make_async_copy(tr, tr_h, whole_sem.at[0]),
        pltpu.make_async_copy(surf, s_h, whole_sem.at[1]),
    ]
    for c in copies:
        c.start()
    per = rows // QUARTERS
    for q in range(QUARTERS):

        @pl.loop(0, per // 8)
        def _(g):
            rs = pl.ds(pl.multiple_of(q * per + g * 8, 8), 8)
            x, y = gx[rs, :], gy[rs, :]
            for l in range(lev):
                w = wet[l, rs, :]
                u[l, rs, :] = w * (us[l, rs, :] - x)
                v[l, rs, :] = w * (vs[l, rs, :] - y)

        part = pl.ds(q * per, per)
        for i, (src, dst) in enumerate(((u, u_h), (v, v_h))):
            c = pltpu.make_async_copy(src.at[:, part], dst.at[:, part], part_sem.at[2 * q + i])
            c.start()
            copies.append(c)
    for c in copies:
        c.wait()


def on_device(nlon, nlat, tracer, u_vel, v_vel, surface, land_mask, bottom, w_in, b_in, w_mid, b_mid, w_out):
    lev, rows, cols = tracer.shape
    hid = w_mid.shape[0]
    ext = (rows + 16, cols + 128)
    cube = jax.ShapeDtypeStruct(tracer.shape, F32)
    vmem = pl.BlockSpec(memory_space=pltpu.VMEM)
    args = (tracer, u_vel, v_vel, surface, land_mask, bottom, w_in, b_in[None], w_mid, b_mid[None], w_out.T)
    plane = jax.ShapeDtypeStruct(surface.shape, F32)
    hbm = pl.BlockSpec(memory_space=pltpu.HBM)
    strip = 32 + 2 * lev
    scratch = (
        [pltpu.VMEM(a.shape, a.dtype) for a in args]
        + [pltpu.VMEM(tracer.shape, F32)] * 2
        + [pltpu.VMEM(ext, F32)] * 7
        + [
            pltpu.VMEM((8 * hid, 24 * lev), BF16),
            pltpu.VMEM((hid, hid), BF16),
            pltpu.VMEM((8 * lev, 8 * hid), BF16),
            pltpu.VMEM((hid, cols), F32),
            pltpu.VMEM((hid, cols), F32),
            pltpu.VMEM((8 * hid, cols), BF16),
            pltpu.VMEM((8 * hid, cols), BF16),
        ]
        + [pltpu.VMEM((rows, 128), F32)] * 2
        + [pltpu.VMEM((strip, cols), F32)] * 2
        + [pltpu.VMEM((rows + 16, 128), F32)] * 2
        + [pltpu.VMEM((strip, cols), F32)] * 2
        + [pltpu.VMEM((nlon * nlat, 8, 128), F32)]
        + [pltpu.SemaphoreType.DMA((7,)), pltpu.SemaphoreType.DMA((4 * QUARTERS,))]
        + [pltpu.SemaphoreType.DMA((8,))] * 2
        + [pltpu.SemaphoreType.DMA((nlon * nlat,))] * 2
    )
    held = pl.pallas_call(
        functools.partial(kernel, nlon, nlat),
        out_shape=(cube, cube, cube, plane, cube, plane, plane),
        in_specs=[hbm] * 11,
        out_specs=(vmem,) * 7,
        scratch_shapes=scratch,
        compiler_params=pltpu.CompilerParams(
            collective_id=0, has_side_effects=True, vmem_limit_bytes=40 * 2**20),
    )(*[pltpu.with_memory_space_constraint(a, pltpu.HBM) for a in args])
    return pl.pallas_call(
        finish,
        out_shape=(cube, cube, cube, plane),
        in_specs=[vmem] * 7,
        out_specs=(hbm,) * 4,
        scratch_shapes=[pltpu.VMEM(tracer.shape, F32)] * 2
        + [pltpu.SemaphoreType.DMA((2,)), pltpu.SemaphoreType.DMA((2 * QUARTERS,))],
        compiler_params=pltpu.CompilerParams(vmem_limit_bytes=40 * 2**20),
    )(*held)


def solution(mesh):
    cube, plane = P(None, "lat", "lon"), P("lat", "lon")
    return jax.shard_map(
        functools.partial(on_device, mesh.shape["lon"], mesh.shape["lat"]),
        mesh=mesh,
        in_specs=(cube, cube, cube, plane, cube, plane, P(), P(), P(), P(), P()),
        out_specs=(cube, cube, cube, plane),
        check_vma=False,
    )
```
